256 devices in a mesh: pipe: 16 (over x, z_hi, core), expert: 16 (over y, z_lo).
Axes of the slice: x: 4, y: 4, z: 8 (z_hi: 2, z_lo: 4; z = z_hi * 4 + z_lo), core: 2. Of those that a mesh axis runs over, the one named last changes fastest.
Arguments:
- tokens: bfloat16 [16, 2048, 1440], P('pipe', 'expert'), may hold values from -6 to 6
- routes_fwd: int32 [16, 2048, 4], P('pipe', 'expert'), may hold values from 0 to 7, all different within a row; in each aligned block of 128 rows (0 to 127, 128 to 255, ..., all dimensions but the last counted through in order) at most 68 rows name the same one
- probs_fwd: float32 [16, 2048, 4], P('pipe', 'expert'), may hold values from 0.1 to 0.6
- grad_out: bfloat16 [16, 2048, 1440], P('pipe', 'expert'), may hold values from -6 to 6
- routes_bwd: int32 [16, 2048, 4], P('pipe', 'expert'), may hold values from 0 to 7, all different within a row; in each aligned block of 128 rows (0 to 127, 128 to 255, ..., all dimensions but the last counted through in order) at most 68 rows name the same one
- probs_bwd: float32 [16, 2048, 4], P('pipe', 'expert'), may hold values from 0.1 to 0.6
- w_in: bfloat16 [16, 16, 1440, 1440], P('pipe', 'expert'), may hold values from -0.15625 to 0.15625
- w_down: bfloat16 [16, 16, 720, 1440], P('pipe', 'expert'), may hold values from -0.15625 to 0.15625
- saved_codes: bfloat16 [16, 17408, 1440], P('pipe', 'expert'), may hold values from -6 to 6
- saved_scales: bfloat16 [16, 17408, 90], P('pipe', 'expert'), may hold values from 0.039794922 to 0.3984375
- saved_exponent: int32 [16, 16], P('pipe', 'expert'), may hold values from -2 to 1
Outputs:
- moe_out: bfloat16 [16, 2048, 1440], P('pipe', 'expert')
- grad_in: bfloat16 [16, 2048, 1440], P('pipe', 'expert')
The draws below stay inside these ranges and needn't reach their ends.
Inputs may be any that keep to these rules, and one draw needn't show every extreme that they name: `routes_fwd`: each row names 4 different experts; over the rows of one device no expert is named more than 68 times, and in every draw some device names some expert exactly 68 times. `routes_bwd`: each row names 4 different experts; over the rows of one device no expert is named more than 68 times, and in every draw some device names some expert exactly 68 times.
All inputs are finite; a program needn't handle non-finite values.
Results may differ from the reference program's by a relative error of at most 0.0065.
Values may be sent and summed in bfloat16 or wider, within the bound.
A program may use at most 128 MiB of HBM per device.

```python
import math
import jax
import jax.numpy as jnp
import numpy as np
from jax import lax

D = 1440
FF = 1440
TOPK = 4
BLOCK = 16
TOK_DEV = 128
TOKENS = 2048
EXPERTS = 8
UNITS = 720
CAP = 68
ROWS = 1088
SCALES = 90
N_PIPE = 16
N_EXPERT = 16


def place_ends(drawn, key, low, largest):
    shape = drawn.shape
    index_at = [jax.random.randint(jax.random.fold_in(key, axis), (), 0, shape[axis]) for axis in range(len(shape))]
    drawn = drawn.at[tuple(index_at)].set(low)
    longest = shape.index(max(shape))
    index_at[longest] = (index_at[longest] + 1) % shape[longest]
    return drawn.at[tuple(index_at)].set(largest)


def block_scale(key, shape, cuts, smallest, high):
    factor_of = 1.0
    for dim, shards_of in cuts:
        draws = jax.random.uniform(jax.random.fold_in(jax.random.fold_in(key, 6), dim), (shards_of,), jnp.float32, smallest / len(cuts), high / len(cuts))
        factor_of = factor_of * jnp.repeat(jnp.exp(draws), shape[dim] // shards_of).reshape((-1,) + (1,) * (len(shape) - 1 - dim))
    return factor_of


def shared_out(key, own, number, rows, amount, top, most, skew):
    ranking = jax.random.permutation(key, amount)
    heavy_load, common = load_shares(amount, rows * top, most, skew, True), load_shares(amount, rows * top, most, skew, False)
    places = jnp.arange(amount)

    def named(lengths, turn):
        used = int((lengths > 0).sum())
        fixed = max(1, used // 4)
        shifted = fixed + (places - fixed + turn * (used - fixed)) % max(1, amount - fixed)
        return jnp.zeros((amount,), jnp.int32).at[ranking[jnp.where(places < fixed, places, shifted)]].set(jnp.asarray(lengths, jnp.int32))

    lengths = jnp.where(number % 4 == 0, named(heavy_load, number // 4), named(common, number - number // 4 - 1))
    mixed = jax.random.permutation(jax.random.fold_in(own, 3), amount)
    source_of, sink = mixed[0:amount // 2 * 2:2], mixed[1:amount // 2 * 2:2]
    margin = jnp.minimum(lengths[source_of] - 1, most - lengths[sink]) // 2
    margin = jnp.where((source_of == ranking[0]) | (sink == ranking[0]) | (lengths[sink] == 0), 0, jnp.maximum(margin, 0))
    shifted = jax.random.randint(jax.random.fold_in(own, 4), (amount // 2,), 0, 1 << 20) % (margin + 1)
    lengths = lengths.at[source_of].add(-shifted).at[sink].add(shifted)
    items = jnp.searchsorted(jnp.cumsum(lengths), jnp.arange(rows * top), side="right").astype(jnp.int32)
    table = items.reshape(top, rows).T
    table = table[jax.random.permutation(jax.random.fold_in(own, 1), rows)]
    turn = jax.random.randint(jax.random.fold_in(own, 2), (rows, 1), 0, top)
    return jnp.take_along_axis(table, (jnp.arange(top)[None, :] + turn) % top, axis=1)


def load_shares(number_of, total, most, slope, full):
    portions = [(1 << 20) // math.isqrt(standing ** slope) + 1 for standing in range(1, number_of + 1)]
    largest = most if full else min(most, max(-(-total // number_of), total * portions[0] // sum(portions)))
    least = 1 if total - largest >= number_of - 1 else 0
    counts, rest = [largest] + [least] * (number_of - 1), total - largest - least * (number_of - 1)
    while rest > 0:
        movable = [i for i in range(1, number_of) if counts[i] < largest] or [i for i in range(1, number_of) if counts[i] < most]
        mass, remaining = sum([portions[i] for i in movable]), rest
        for i in movable:
            more = min(most - counts[i], max(1, remaining * portions[i] // mass), rest)
            counts[i] = counts[i] + more
            rest = rest - more
    return np.array(counts)


def normal_values(rng, dims, deviation, bound, shards=(), kind=jnp.bfloat16):
    array = deviation * jax.random.normal(rng, dims, jnp.float32)
    if shards:
        array = array * block_scale(rng, dims, shards, -0.22, 0.18)
    return jnp.clip(array, -bound, bound).astype(kind)


def setup_inputs(seed: int = 0) -> dict:
    key_list = jax.random.split(jax.random.key(seed), 12)
    tokens = normal_values(key_list[0], (N_PIPE, TOKENS, D), 1.0, 6.0, ((0, 16), (1, 16)))
    routes_fwd_keys = jax.random.split(jax.random.fold_in(key_list[1], 1), N_PIPE * TOKENS // TOK_DEV)
    routes_fwd_turns = jax.random.permutation(jax.random.fold_in(key_list[1], 3), N_PIPE * TOKENS // TOK_DEV)
    routes_fwd = jax.vmap(lambda own, number: shared_out(jax.random.fold_in(key_list[1], 2), own, number, TOK_DEV, EXPERTS, TOPK, CAP, 1))(routes_fwd_keys, routes_fwd_turns).reshape((N_PIPE, TOKENS, TOPK))
    probs_fwd = jnp.clip(jnp.exp(math.log(0.6) - 1.7917595 * jax.random.uniform(key_list[2], (N_PIPE, TOKENS, TOPK), jnp.float32) ** block_scale(key_list[2], (N_PIPE, TOKENS, TOPK), ((0, 16), (1, 16)), -0.2, 0.2)), 0.1, 0.6)
    grad_out = normal_values(key_list[3], (N_PIPE, TOKENS, D), 1.0, 6.0, ((0, 16), (1, 16)))
    routes_bwd_keys = jax.random.split(jax.random.fold_in(key_list[4], 1), N_PIPE * TOKENS // TOK_DEV)
    routes_bwd_turns = jax.random.permutation(jax.random.fold_in(key_list[4], 3), N_PIPE * TOKENS // TOK_DEV)
    routes_bwd = jax.vmap(lambda own, number: shared_out(jax.random.fold_in(key_list[4], 2), own, number, TOK_DEV, EXPERTS, TOPK, CAP, 1))(routes_bwd_keys, routes_bwd_turns).reshape((N_PIPE, TOKENS, TOPK))
    probs_bwd = jnp.clip(jnp.exp(math.log(0.6) - 1.7917595 * jax.random.uniform(key_list[5], (N_PIPE, TOKENS, TOPK), jnp.float32) ** block_scale(key_list[5], (N_PIPE, TOKENS, TOPK), ((0, 16), (1, 16)), -0.2, 0.2)), 0.1, 0.6)
    w_in = normal_values(key_list[6], (N_PIPE, N_EXPERT, D, 2 * UNITS), D ** -0.5, 0.15625, ((0, 16), (1, 16)))
    w_down = normal_values(key_list[7], (N_PIPE, N_EXPERT, UNITS, D), FF ** -0.5, 0.15625, ((0, 16), (1, 16)))
    saved_codes = jnp.clip(jax.random.uniform(key_list[8], (N_PIPE, N_EXPERT * ROWS, 2 * UNITS), jnp.float32, -6.0, 6.0) * block_scale(key_list[8], (N_PIPE, N_EXPERT * ROWS, 2 * UNITS), ((0, 16), (1, 16)), -0.4, 0.0), -6.0, 6.0).astype(jnp.bfloat16)
    saved_scales = jnp.clip(jnp.exp(math.log(0.3984375) - 2.3038113 * jax.random.uniform(key_list[9], (N_PIPE, N_EXPERT * ROWS, SCALES), jnp.float32) ** block_scale(key_list[9], (N_PIPE, N_EXPERT * ROWS, SCALES), ((0, 16), (1, 16)), -0.2, 0.2)), 0.039794922, 0.3984375).astype(jnp.bfloat16)
    saved_exponent = place_ends(jax.random.randint(key_list[10], (N_PIPE, N_EXPERT), -2, 2), jax.random.fold_in(key_list[10], 1), -2, 1).astype(jnp.int32)
    return {"tokens": tokens, "routes_fwd": routes_fwd, "probs_fwd": probs_fwd, "grad_out": grad_out, "routes_bwd": routes_bwd, "probs_bwd": probs_bwd, "w_in": w_in, "w_down": w_down, "saved_codes": saved_codes, "saved_scales": saved_scales, "saved_exponent": saved_exponent}


def power_two(exponent):
    running = jnp.zeros(exponent.shape, jnp.float32)
    for exponent_level in range(-2, 2):
        running = running + jnp.where(exponent == exponent_level, jnp.float32(2.0 ** exponent_level), jnp.float32(0.0))
    return running


def slot_positions(routes):
    expert_ids = routes.reshape(N_EXPERT, TOK_DEV * TOPK)
    onehot = (expert_ids[:, :, None] == jnp.arange(EXPERTS, dtype=jnp.int32)[None, None, :]).astype(jnp.int32)
    before = jnp.cumsum(onehot, axis=1) - onehot
    slot_index = jnp.sum(before * onehot, axis=2).astype(jnp.int32)
    return expert_ids, slot_index


def place_rows(row_data, expert_ids, slot_index):
    source = jnp.broadcast_to(jnp.arange(N_EXPERT, dtype=jnp.int32)[:, None], expert_ids.shape)
    buffer = jnp.zeros((N_EXPERT, EXPERTS, CAP, D), jnp.bfloat16)
    return buffer.at[source, expert_ids, slot_index].set(row_data)


def pick_pairs(results, expert_ids, slot_index):
    source = jnp.broadcast_to(jnp.arange(N_EXPERT, dtype=jnp.int32)[:, None], expert_ids.shape)
    shaped = results.reshape(EXPERTS, 2, N_EXPERT, CAP, D)
    first_half = shaped[expert_ids, 0, source, slot_index].astype(jnp.float32)
    second = shaped[expert_ids, 1, source, slot_index].astype(jnp.float32)
    return first_half + second


def reference(tokens, routes_fwd, probs_fwd, grad_out, routes_bwd, probs_bwd, w_in, w_down, saved_codes, saved_scales, saved_exponent):
    held_codes = jnp.flip(saved_codes, 0)
    held_scales = jnp.flip(saved_scales, 0)
    held_exponent = jnp.flip(saved_exponent, 0)

    def section(section_inputs):
        tok_data, route_now, prob_now, grad_data, route_old, prob_old, section_in, section_down, codes_held, scales_held, exponent_held = section_inputs
        ids_now, slots_now = slot_positions(route_now)
        rows_now = jnp.repeat(tok_data.reshape(N_EXPERT, TOK_DEV, D), TOPK, axis=1)
        buffer_now = place_rows(rows_now, ids_now, slots_now)

        def expert_forward(device):
            inputs = lax.dynamic_index_in_dim(buffer_now, device // 2, 1, False).reshape(ROWS, D)
            weight_in = lax.dynamic_index_in_dim(section_in, device, 0, False)
            weight_down = lax.dynamic_index_in_dim(section_down, device, 0, False)
            gate_up = jnp.dot(inputs, weight_in, preferred_element_type=jnp.float32)
            hidden = (jax.nn.silu(gate_up[:, :UNITS]) * gate_up[:, UNITS:]).astype(jnp.bfloat16)
            return jnp.dot(hidden, weight_down, preferred_element_type=jnp.float32).astype(jnp.bfloat16)

        outputs = lax.map(expert_forward, jnp.arange(N_EXPERT, dtype=jnp.int32))
        pairs = pick_pairs(outputs, ids_now, slots_now)
        weighted = prob_now.reshape(N_EXPERT, TOK_DEV * TOPK, 1).astype(jnp.float32) * pairs
        moe_out = jnp.sum(weighted.reshape(N_EXPERT, TOK_DEV, TOPK, D), axis=2).reshape(TOKENS, D).astype(jnp.bfloat16)

        ids_old, slots_old = slot_positions(route_old)
        rows_old = jnp.repeat(grad_data.reshape(N_EXPERT, TOK_DEV, D).astype(jnp.float32), TOPK, axis=1)
        rows_old = (rows_old * prob_old.reshape(N_EXPERT, TOK_DEV * TOPK, 1).astype(jnp.float32)).astype(jnp.bfloat16)
        buffer_old = place_rows(rows_old, ids_old, slots_old)

        def expert_backward(device):
            grad_rows = lax.dynamic_index_in_dim(buffer_old, device // 2, 1, False).reshape(ROWS, D)
            weight_in = lax.dynamic_index_in_dim(section_in, device, 0, False)
            weight_down = lax.dynamic_index_in_dim(section_down, device, 0, False)
            saved_rows = lax.dynamic_slice_in_dim(codes_held, device * ROWS, ROWS, 0)
            block_rows = lax.dynamic_slice_in_dim(scales_held, device * ROWS, ROWS, 0)
            factor = power_two(lax.dynamic_index_in_dim(exponent_held, device, 0, False)).astype(jnp.bfloat16)
            block_rows = block_rows * factor
            values = saved_rows.reshape(ROWS, SCALES, BLOCK).astype(jnp.float32) * block_rows.astype(jnp.float32)[:, :, None]
            values = values.reshape(ROWS, 2 * UNITS)
            gate_part = values[:, :UNITS]
            up_part = values[:, UNITS:]
            hidden_grad = lax.dot_general(grad_rows, weight_down, (((1,), (1,)), ((), ())), preferred_element_type=jnp.float32)
            sigmoid_gate = jax.nn.sigmoid(gate_part)
            gate_grad = (hidden_grad * up_part * sigmoid_gate * (1.0 + gate_part * (1.0 - sigmoid_gate))).astype(jnp.bfloat16)
            up_grad = (hidden_grad * gate_part * sigmoid_gate).astype(jnp.bfloat16)
            joined = jnp.concatenate([gate_grad, up_grad], axis=1)
            return lax.dot_general(joined, weight_in, (((1,), (1,)), ((), ())), preferred_element_type=jnp.float32).astype(jnp.bfloat16)

        input_rows = lax.map(expert_backward, jnp.arange(N_EXPERT, dtype=jnp.int32))
        grad_pairs = pick_pairs(input_rows, ids_old, slots_old)
        grad_in = jnp.sum(grad_pairs.reshape(N_EXPERT, TOK_DEV, TOPK, D), axis=2).reshape(TOKENS, D).astype(jnp.bfloat16)
        return moe_out, grad_in

    moe_out, grad_in = lax.map(section, (tokens, routes_fwd, probs_fwd, grad_out, routes_bwd, probs_bwd, w_in, w_down, held_codes, held_scales, held_exponent))
    return (moe_out, grad_in)
```

```python
import functools
import jax
import jax.numpy as jnp
from jax import lax
from jax.sharding import PartitionSpec as P
from jax.experimental import pallas as pl
from jax.experimental.pallas import tpu as pltpu

MESH = pl.DeviceIdType.MESH
LINE = 4
BF16 = jnp.bfloat16
F32 = jnp.float32


def dot(a, b, dims=((1,), (0,))):
    return lax.dot_general(a, b, (dims, ((), ())), preferred_element_type=F32)


def kernel(
    sizes,
    table_ref,
    tok_ref,
    grad_ref,
    win_ref,
    wdown_ref,
    codes_ref,
    scales_ref,
    exp_ref,
    moe_ref,
    gin_ref,
    tabs,
    gathered,
    target,
    weight,
    target_t,
    weight_t,
    coef_out,
    coef_in,
    rows_out,
    rows_in,
    back_in,
    total,
    part_out,
    part_up,
    part_down,
    tab_send,
    tab_recv,
    tok_send,
    tok_recv,
    coef_send,
    coef_recv,
    rows_send,
    rows_recv,
    back_send,
    back_recv,
    part_send,
    up_recv,
    down_recv,
):
    pipes, planes, cap, chunk, tok, units, wide, block = sizes
    p = lax.axis_index("pipe")
    e = lax.axis_index("expert")
    y = e // LINE
    z = e % LINE

    def on_z(q):
        return (p, y * LINE + q)

    def on_y(q):
        return (p, q * LINE + z)

    mirror = (pipes - 1 - p, e)

    tabs[z] = table_ref[...]
    gathered[0, z] = tok_ref[...]
    gathered[1, z] = grad_ref[...]

    bar = pltpu.get_barrier_semaphore()
    pl.semaphore_signal(bar, inc=1, device_id=mirror, device_id_type=MESH)
    for i in range(1, planes):
        pl.semaphore_signal(bar, inc=1, device_id=on_y((y + i) % planes), device_id_type=MESH)

    @pl.when(z > 0)
    def _():
        pl.semaphore_signal(bar, inc=1, device_id=on_z(z - 1), device_id_type=MESH)

    @pl.when(z < LINE - 1)
    def _():
        pl.semaphore_signal(bar, inc=1, device_id=on_z(z + 1), device_id_type=MESH)

    @pl.when((z > 0) & (z < LINE - 1))
    def _():
        pl.semaphore_wait(bar, planes + 2)

    @pl.when((z == 0) | (z == LINE - 1))
    def _():
        pl.semaphore_wait(bar, planes + 1)

    def hop_copy(kind, up, zs):
        to = on_z(z + 1) if up else on_z(z - 1)
        way = 0 if up else 1
        if kind == 2:
            return pltpu.make_async_remote_copy(
                tabs.at[zs], tabs.at[zs], tab_send.at[way, zs], tab_recv.at[zs],
                device_id=to, device_id_type=MESH,
            )
        return pltpu.make_async_remote_copy(
            gathered.at[kind, zs], gathered.at[kind, zs], tok_send.at[kind, way, zs],
            tok_recv.at[kind, zs], device_id=to, device_id_type=MESH,
        )

    def hop(kind, d):
        if d == 0:
            @pl.when(z < LINE - 1)
            def _():
                hop_copy(kind, True, z).start()

            @pl.when(z > 0)
            def _():
                hop_copy(kind, False, z).start()
            return

        @pl.when(z >= d)
        def _():
            hop_copy(kind, True, z - d).wait_recv()

            @pl.when(z < LINE - 1)
            def _():
                hop_copy(kind, True, z - d).start()

        @pl.when(z + d <= LINE - 1)
        def _():
            hop_copy(kind, False, z + d).wait_recv()

            @pl.when(z > 0)
            def _():
                hop_copy(kind, False, z + d).start()

    def hop_done(kind):
        for d in range(LINE - 1):
            @pl.when((z < LINE - 1) & (z >= d))
            def _():
                hop_copy(kind, True, z - d).wait_send()

            @pl.when((z > 0) & (z + d <= LINE - 1))
            def _():
                hop_copy(kind, False, z + d).wait_send()

    for kind in (2, 0, 1):
        hop(kind, 0)

    def coef_copy(q):
        return pltpu.make_async_remote_copy(
            coef_out.at[q], coef_in.at[q], coef_send.at[q], coef_recv.at[q],
            device_id=mirror, device_id_type=MESH,
        )

    blocks = scales_ref.shape[1]
    low = lax.broadcasted_iota(jnp.int32, (blocks, 2 * units), 0) * block
    lane = lax.broadcasted_iota(jnp.int32, (blocks, 2 * units), 1)
    spread = jnp.where((lane >= low) & (lane < low + block), 1.0, 0.0).astype(BF16)
    level = exp_ref[...]
    factor = jnp.zeros(level.shape, F32)
    for n in range(-2, 2):
        factor = factor + jnp.where(level == n, F32(2.0**n), F32(0.0))

    def coef_step(i, carry):
        q = (y + 2 * planes - 1 - i) % planes
        r0 = pl.multiple_of(q * chunk, 16)
        scale = dot(scales_ref[pl.ds(r0, chunk), :], spread) * factor
        value = codes_ref[pl.ds(r0, chunk), :].astype(F32) * scale
        gate = value[:, :units]
        up = value[:, units:]
        sig = 1.0 / (1.0 + jnp.exp(-gate))
        coef_out[q, :, 0:units] = (up * sig * (1.0 + gate * (1.0 - sig))).astype(BF16)
        coef_out[q, :, wide : wide + units] = (gate * sig).astype(BF16)

        @pl.when((z == 0) | (z == LINE - 1))
        def _():
            coef_copy(q).start()
        return carry

    lax.fori_loop(0, planes, coef_step, 0)

    for d in (1, 2):
        for kind in (2, 0, 1):
            hop(kind, d)

    @pl.when((z > 0) & (z < LINE - 1))
    def _():
        for i in range(planes):
            coef_copy((y + 2 * planes - 1 - i) % planes).start()

    hop(2, 3)

    plane_expert = (
        2 * lax.broadcasted_iota(jnp.int32, (8, tok), 0) + z // 2
    ).astype(F32)
    earlier = jnp.where(
        lax.broadcasted_iota(jnp.int32, (tok, tok), 0)
        < lax.broadcasted_iota(jnp.int32, (tok, tok), 1),
        1.0,
        0.0,
    ).astype(BF16)
    for ph in range(2):
        for zs in range(LINE):
            member = jnp.zeros((8, tok), F32)
            prob = jnp.zeros((8, tok), F32)
            for k in range(4):
                hit = tabs[zs, 8 * ph + k : 8 * ph + k + 1, :] == plane_expert
                member = member + jnp.where(hit, 1.0, 0.0)
                prob = prob + jnp.where(hit, tabs[zs, 8 * ph + 4 + k : 8 * ph + 5 + k, :], 0.0)
            before = dot(member.astype(BF16), earlier)
            target[ph, :, zs * tok : (zs + 1) * tok] = jnp.where(
                member > 0.5, before + F32(zs * cap), F32(-1.0)
            )
            weight[ph, :, zs * tok : (zs + 1) * tok] = prob
        target_t[ph] = target[ph].T
        weight_t[ph] = weight[ph].T

    def rows_copy(ph, q):
        return pltpu.make_async_remote_copy(
            rows_out.at[ph, q], rows_in.at[ph, y], rows_send.at[ph, q], rows_recv.at[ph, y],
            device_id=on_y(q), device_id_type=MESH,
        )

    def rows_arrived(ph, q):
        return pltpu.make_async_remote_copy(
            rows_out.at[ph, q], rows_in.at[ph, q], rows_send.at[ph, q], rows_recv.at[ph, q],
            device_id=on_y(q), device_id_type=MESH,
        )

    def back_copy(ph, q):
        return pltpu.make_async_remote_copy(
            rows_in.at[ph, q], back_in.at[ph, y], back_send.at[ph, q], back_recv.at[ph, y],
            device_id=on_y(q), device_id_type=MESH,
        )

    def back_arrived(ph, q):
        return pltpu.make_async_remote_copy(
            rows_in.at[ph, q], back_in.at[ph, q], back_send.at[ph, q], back_recv.at[ph, q],
            device_id=on_y(q), device_id_type=MESH,
        )

    line_tok = LINE * tok
    slot_row = lax.broadcasted_iota(jnp.int32, (chunk, line_tok), 0).astype(F32)

    def send_rows(ph):
        def step(i, carry):
            q = (y + 1 + i) % planes
            match = slot_row == target[ph, pl.ds(q, 1), :]
            rows = dot(
                jnp.where(match, 1.0, 0.0).astype(BF16),
                gathered[ph].reshape(line_tok, gathered.shape[-1]),
            )
            if ph == 1:
                rows = rows * jnp.sum(
                    jnp.where(match, weight[ph, pl.ds(q, 1), :], 0.0), axis=1, keepdims=True
                )
            rows_out[ph, q] = rows.astype(BF16)

            @pl.when(i < planes - 1)
            def _():
                rows_copy(ph, q).start()
            return carry

        lax.fori_loop(0, planes, step, 0)
        rows_in[ph, y] = rows_out[ph, y]

    hop(0, 3)
    send_rows(0)
    hop(1, 3)
    send_rows(1)

    def forward_step(i, carry):
        q = (y + planes - i) % planes

        @pl.when(i > 0)
        def _():
            rows_arrived(0, q).wait_recv()

        both = dot(rows_in[0, q], win_ref[...])
        gate = both[:, :units]
        hidden = (gate * (1.0 / (1.0 + jnp.exp(-gate))) * both[:, units:]).astype(BF16)
        rows_in[0, q] = dot(hidden, wdown_ref[...]).astype(BF16)

        @pl.when(i > 0)
        def _():
            back_copy(0, q).start()
        return carry

    lax.fori_loop(0, planes, forward_step, 0)

    lane_row = lax.broadcasted_iota(jnp.int32, (line_tok, chunk), 1).astype(F32)
    column = lax.broadcasted_iota(jnp.int32, (line_tok, 8), 1)

    def combine(ph):
        back_in[ph, y] = rows_in[ph, y]
        total[ph] = jnp.zeros(total.shape[1:], F32)

        def step(i, carry):
            q = (y + i) % planes

            @pl.when(i > 0)
            def _():
                back_arrived(ph, q).wait_recv()

            place = jnp.sum(jnp.where(column == q, target_t[ph], 0.0), axis=1, keepdims=True)
            match = lane_row == place
            rows = back_in[ph, q]
            if ph == 0:
                prob = jnp.sum(jnp.where(column == q, weight_t[ph], 0.0), axis=1, keepdims=True)
                full = jnp.where(match, prob, 0.0)
                high = full.astype(BF16)
                rest = (full - high.astype(F32)).astype(BF16)
                value = dot(high, rows) + dot(rest, rows)
            else:
                value = dot(jnp.where(match, 1.0, 0.0).astype(BF16), rows)
            total[ph] += value.reshape(total.shape[1:])
            return carry

        lax.fori_loop(0, planes, step, 0)

    def part_copy(ph, up, d):
        if up:
            return pltpu.make_async_remote_copy(
                part_out.at[ph, d], part_up.at[ph, d], part_send.at[ph, d], up_recv.at[ph, d],
                device_id=on_z(z + 1), device_id_type=MESH,
            )
        return pltpu.make_async_remote_copy(
            part_out.at[ph, d], part_down.at[ph, d], part_send.at[ph, d], down_recv.at[ph, d],
            device_id=on_z(z - 1), device_id_type=MESH,
        )

    def send_up(ph, d):
        @pl.when(z == 0)
        def _():
            part_out[ph, d] = total[ph, d].astype(BF16)

        @pl.when((z > 0) & (z < d))
        def _():
            part_copy(ph, True, d).wait_recv()
            part_out[ph, d] = (total[ph, d] + part_up[ph, d].astype(F32)).astype(BF16)

        @pl.when(z < d)
        def _():
            part_copy(ph, True, d).start()

    def send_down(ph, d):
        @pl.when(z == LINE - 1)
        def _():
            part_out[ph, d] = total[ph, d].astype(BF16)

        @pl.when((z < LINE - 1) & (z > d))
        def _():
            part_copy(ph, False, d).wait_recv()
            part_out[ph, d] = (total[ph, d] + part_down[ph, d].astype(F32)).astype(BF16)

        @pl.when(z > d)
        def _():
            part_copy(ph, False, d).start()

    def reduce_line(ph):
        for s in range(LINE - 1):
            @pl.when((z > 0) & (z < LINE // 2))
            def _():
                send_up(ph, LINE - 1 - s)
                send_down(ph, s)

            @pl.when((z >= LINE // 2) & (z < LINE - 1))
            def _():
                send_down(ph, s)
                send_up(ph, LINE - 1 - s)

    def reduce_ends(ph):
        @pl.when(z == 0)
        def _():
            for s in range(LINE - 1):
                send_up(ph, LINE - 1 - s)

        @pl.when(z == LINE - 1)
        def _():
            for s in range(LINE - 1):
                send_down(ph, s)

    def finish_line(ph, out_ref):
        @pl.when(z > 0)
        def _():
            part_copy(ph, True, z).wait_recv()
            total[ph, z] += part_up[ph, z].astype(F32)

        @pl.when(z < LINE - 1)
        def _():
            part_copy(ph, False, z).wait_recv()
            total[ph, z] += part_down[ph, z].astype(F32)

        out_ref[...] = total[ph, z].astype(BF16)

    combine(0)

    reduce_ends(0)

    def backward_step(i, carry):
        q = (y + 2 * planes - 1 - i) % planes

        @pl.when(i < planes - 1)
        def _():
            rows_arrived(1, q).wait_recv()

        hidden = dot(rows_in[1, q], wdown_ref[...], ((1,), (1,)))
        coef_copy(q).wait_recv()
        joined = jnp.concatenate(
            [
                hidden * coef_in[q, :, 0:units].astype(F32),
                hidden * coef_in[q, :, wide : wide + units].astype(F32),
            ],
            axis=1,
        ).astype(BF16)
        rows_in[1, q] = dot(joined, win_ref[...], ((1,), (1,))).astype(BF16)

        @pl.when(i < planes - 1)
        def _():
            back_copy(1, q).start()
        return carry

    lax.fori_loop(0, planes, backward_step, 0)
    combine(1)
    reduce_ends(1)
    reduce_line(0)
    reduce_line(1)
    finish_line(0, moe_ref)
    finish_line(1, gin_ref)

    for kind in range(3):
        hop_done(kind)
    for q in range(planes):
        coef_copy(q).wait_send()
    for ph in range(2):
        for i in range(1, planes):
            rows_copy(ph, (y + i) % planes).wait_send()
            back_copy(ph, (y + i) % planes).wait_send()
        for d in range(LINE):
            @pl.when(z < d)
            def _():
                part_copy(ph, True, d).wait_send()

            @pl.when(z > d)
            def _():
                part_copy(ph, False, d).wait_send()


def local(
    tokens,
    routes_fwd,
    probs_fwd,
    grad_out,
    routes_bwd,
    probs_bwd,
    w_in,
    w_down,
    saved_codes,
    saved_scales,
    saved_exponent,
):
    devices = lax.axis_size("expert")
    planes = devices // LINE
    tok, depth = tokens.shape[1:]
    units = w_down.shape[2]
    rows = saved_codes.shape[1]
    cap = rows // devices
    chunk = cap * LINE
    wide = -(-units // 128) * 128
    block = 2 * units // saved_scales.shape[2]
    table = jnp.concatenate(
        [
            routes_fwd[0].astype(F32),
            probs_fwd[0],
            routes_bwd[0].astype(F32),
            probs_bwd[0],
        ],
        axis=1,
    ).T
    sizes = (lax.axis_size("pipe"), planes, cap, chunk, tok, units, wide, block)
    vmem = pl.BlockSpec(memory_space=pltpu.VMEM)
    dma = pltpu.SemaphoreType.DMA
    moe, gin = pl.pallas_call(
        functools.partial(kernel, sizes),
        out_shape=[jax.ShapeDtypeStruct((tok, depth), BF16)] * 2,
        in_specs=[vmem] * 8,
        out_specs=[vmem] * 2,
        scratch_shapes=[
            pltpu.VMEM((LINE, 16, tok), F32),
            pltpu.VMEM((2, LINE, tok, depth), BF16),
            pltpu.VMEM((2, 8, LINE * tok), F32),
            pltpu.VMEM((2, 8, LINE * tok), F32),
            pltpu.VMEM((2, LINE * tok, 8), F32),
            pltpu.VMEM((2, LINE * tok, 8), F32),
            pltpu.VMEM((planes, chunk, 2 * wide), BF16),
            pltpu.VMEM((planes, chunk, 2 * wide), BF16),
            pltpu.VMEM((2, planes, chunk, depth), BF16),
            pltpu.VMEM((2, planes, chunk, depth), BF16),
            pltpu.VMEM((2, planes, chunk, depth), BF16),
            pltpu.VMEM((2, LINE, tok, depth), F32),
            pltpu.VMEM((2, LINE, tok, depth), BF16),
            pltpu.VMEM((2, LINE, tok, depth), BF16),
            pltpu.VMEM((2, LINE, tok, depth), BF16),
            dma((2, LINE)),
            dma((LINE,)),
            dma((2, 2, LINE)),
            dma((2, LINE)),
            dma((planes,)),
            dma((planes,)),
            dma((2, planes)),
            dma((2, planes)),
            dma((2, planes)),
            dma((2, planes)),
            dma((2, LINE)),
            dma((2, LINE)),
            dma((2, LINE)),
        ],
        compiler_params=pltpu.CompilerParams(
            collective_id=0, has_side_effects=True, vmem_limit_bytes=62 << 20
        ),
        cost_estimate=pl.CostEstimate(
            flops=8 * rows * units * depth * 3, bytes_accessed=16 << 20, transcendentals=0
        ),
    )(
        table,
        tokens[0],
        grad_out[0],
        w_in[0, 0],
        w_down[0, 0],
        saved_codes[0],
        saved_scales[0],
        saved_exponent,
    )
    return (moe[None], gin[None])


def solution(mesh):
    rows3 = P("pipe", "expert", None)
    rows4 = P("pipe", "expert", None, None)
    in_specs = (rows3,) * 6 + (rows4, rows4, rows3, rows3, P("pipe", "expert"))
    return jax.shard_map(
        local, mesh=mesh, in_specs=in_specs, out_specs=(rows3, rows3), check_vma=False
    )
```

```python
import functools
import jax
import jax.numpy as jnp
from jax import lax
from jax.sharding import PartitionSpec as P
from jax.experimental import pallas as pl
from jax.experimental.pallas import tpu as pltpu

MESH = pl.DeviceIdType.MESH
LINE = 4
BF16 = jnp.bfloat16
F32 = jnp.float32


def dot(a, b, dims=((1,), (0,))):
    return lax.dot_general(a, b, (dims, ((), ())), preferred_element_type=F32)


def kernel(
    sizes,
    route_now_ref,
    prob_now_ref,
    route_old_ref,
    prob_old_ref,
    tok_ref,
    grad_ref,
    win_hbm,
    wdown_hbm,
    codes_hbm,
    scales_ref,
    exp_ref,
    moe_ref,
    gin_ref,
    win_ref,
    wdown_ref,
    codes_ref,
    final,
    rest_all,
    load_sem,
    tabs,
    gathered,
    target,
    weight,
    target_t,
    weight_t,
    coef_out,
    coef_in,
    rest_out,
    rest_in,
    rows_out,
    rows_in,
    back_in,
    total,
    part_out,
    part_up,
    part_down,
    tab_send,
    tab_recv,
    tok_send,
    tok_recv,
    coef_send,
    coef_recv,
    rest_send,
    rest_recv,
    rows_send,
    rows_recv,
    back_send,
    back_recv,
    part_send,
    up_recv,
    down_recv,
):
    pipes, planes, cap, chunk, tok, units, block = sizes
    main = units // 128 * 128
    body = 2 * units // 128 * 128
    rest = 2 * units - body
    p = lax.axis_index("pipe")
    e = lax.axis_index("expert")
    y = e // LINE
    z = e % LINE

    def on_z(q):
        return (p, y * LINE + q)

    def on_y(q):
        return (p, q * LINE + z)

    mirror = (pipes - 1 - p, e)

    loads = [
        pltpu.make_async_copy(src, dst, load_sem.at[n])
        for n, (src, dst) in enumerate(
            ((codes_hbm, codes_ref), (win_hbm, win_ref), (wdown_hbm, wdown_ref))
        )
    ]
    for load in loads:
        load.start()

    for n, part in enumerate((route_now_ref, prob_now_ref, route_old_ref, prob_old_ref)):
        tabs[z, 4 * n : 4 * n + 4, :] = part[...].astype(F32)
    gathered[0, z] = tok_ref[...]
    gathered[1, z] = grad_ref[...]

    bar = pltpu.get_barrier_semaphore()
    pl.semaphore_signal(bar, inc=1, device_id=mirror, device_id_type=MESH)
    for i in range(1, planes):
        pl.semaphore_signal(bar, inc=1, device_id=on_y((y + i) % planes), device_id_type=MESH)

    @pl.when(z > 0)
    def _():
        pl.semaphore_signal(bar, inc=1, device_id=on_z(z - 1), device_id_type=MESH)

    @pl.when(z < LINE - 1)
    def _():
        pl.semaphore_signal(bar, inc=1, device_id=on_z(z + 1), device_id_type=MESH)

    @pl.when((z > 0) & (z < LINE - 1))
    def _():
        pl.semaphore_wait(bar, planes + 2)

    @pl.when((z == 0) | (z == LINE - 1))
    def _():
        pl.semaphore_wait(bar, planes + 1)

    def hop_copy(kind, up, zs):
        to = on_z(z + 1) if up else on_z(z - 1)
        way = 0 if up else 1
        if kind == 2:
            return pltpu.make_async_remote_copy(
                tabs.at[zs], tabs.at[zs], tab_send.at[way, zs], tab_recv.at[zs],
                device_id=to, device_id_type=MESH,
            )
        return pltpu.make_async_remote_copy(
            gathered.at[kind, zs], gathered.at[kind, zs], tok_send.at[kind, way, zs],
            tok_recv.at[kind, zs], device_id=to, device_id_type=MESH,
        )

    def hop(kind, d):
        if d == 0:
            @pl.when(z < LINE - 1)
            def _():
                hop_copy(kind, True, z).start()

            @pl.when(z > 0)
            def _():
                hop_copy(kind, False, z).start()
            return

        @pl.when(z >= d)
        def _():
            hop_copy(kind, True, z - d).wait_recv()

            @pl.when(z < LINE - 1)
            def _():
                hop_copy(kind, True, z - d).start()

        @pl.when(z + d <= LINE - 1)
        def _():
            hop_copy(kind, False, z + d).wait_recv()

            @pl.when(z > 0)
            def _():
                hop_copy(kind, False, z + d).start()

    def hop_done(kind):
        for d in range(LINE - 1):
            @pl.when((z < LINE - 1) & (z >= d))
            def _():
                hop_copy(kind, True, z - d).wait_send()

            @pl.when((z > 0) & (z + d <= LINE - 1))
            def _():
                hop_copy(kind, False, z + d).wait_send()

    inner = (z > 0) & (z < LINE - 1)
    ends = (z == 0) | (z == LINE - 1)
    hop(2, 0)
    hop(0, 0)

    @pl.when(ends)
    def _():
        hop(1, 0)

    def coef_copy(q):
        return pltpu.make_async_remote_copy(
            coef_out.at[pl.ds(pl.multiple_of(q * chunk, 16), chunk)], coef_in.at[q], coef_send.at[q], coef_recv.at[q],
            device_id=mirror, device_id_type=MESH,
        )

    blocks = scales_ref.shape[0]
    low = lax.broadcasted_iota(jnp.int32, (2 * units, blocks), 1) * block
    line = lax.broadcasted_iota(jnp.int32, (2 * units, blocks), 0)
    spread = jnp.where((line >= low) & (line < low + block), 1.0, 0.0).astype(BF16)
    level = exp_ref[...]
    factor = jnp.zeros(level.shape, F32)
    for n in range(-2, 2):
        factor = factor + jnp.where(level == n, F32(2.0**n), F32(0.0))

    def coef_tile(start, size):
        here = pl.ds(start, size)
        value = codes_ref[:, here].astype(F32) * (dot(spread, scales_ref[:, here]) * factor)
        gate = value[:units]
        up = value[units:]
        sig = 1.0 / (1.0 + jnp.exp(-gate))
        one = (up * sig * (1.0 + gate * (1.0 - sig))).T
        two = (gate * sig).T
        coef_out[here, 0:main] = one[:, :main].astype(BF16)
        coef_out[here, main : 2 * main] = two[:, :main].astype(BF16)
        ending = jnp.concatenate([one[:, main:], two[:, main:]], axis=1)
        coef_out[here, 2 * main : body] = ending[:, : body - 2 * main].astype(BF16)
        rest_all[here, :] = ending[:, body - 2 * main :].astype(BF16)

    def coef_step(t, carry):
        coef_tile(pl.multiple_of(t * 128, 128), 128)
        return carry

    def coef_start(i):
        coef_copy((y + 2 * planes - 1 - i) % planes).start()

    rest_copy = pltpu.make_async_remote_copy(
        rest_out, rest_in, rest_send, rest_recv, device_id=mirror, device_id_type=MESH
    )
    loads[0].wait()
    rows = codes_ref.shape[1]
    half = rows // 256
    lax.fori_loop(0, half, coef_step, 0)
    hop(2, 1)
    hop(0, 1)

    @pl.when(inner)
    def _():
        hop(1, 0)

    lax.fori_loop(half, rows // 128, coef_step, 0)
    if rows % 128:
        coef_tile(rows // 128 * 128, rows % 128)
    rest_out[...] = jnp.concatenate(
        [rest_all[q * chunk : (q + 1) * chunk, :] for q in range(planes)], axis=1
    )

    hop(2, 2)
    hop(0, 2)
    hop(2, 3)

    plane_expert = (
        2 * lax.broadcasted_iota(jnp.int32, (8, tok), 0) + z // 2
    ).astype(F32)
    earlier = jnp.where(
        lax.broadcasted_iota(jnp.int32, (tok, tok), 0)
        < lax.broadcasted_iota(jnp.int32, (tok, tok), 1),
        1.0,
        0.0,
    ).astype(BF16)
    for ph in range(2):
        for zs in range(LINE):
            member = jnp.zeros((8, tok), F32)
            prob = jnp.zeros((8, tok), F32)
            for k in range(4):
                hit = tabs[zs, 8 * ph + k : 8 * ph + k + 1, :] == plane_expert
                member = member + jnp.where(hit, 1.0, 0.0)
                prob = prob + jnp.where(hit, tabs[zs, 8 * ph + 4 + k : 8 * ph + 5 + k, :], 0.0)
            before = dot(member.astype(BF16), earlier)
            target[ph, :, zs * tok : (zs + 1) * tok] = jnp.where(
                member > 0.5, before + F32(zs * cap), F32(-1.0)
            )
            weight[ph, :, zs * tok : (zs + 1) * tok] = prob
        target_t[ph] = target[ph].T
        weight_t[ph] = weight[ph].T

    def rows_copy(ph, q):
        return pltpu.make_async_remote_copy(
            rows_out.at[ph, q], rows_in.at[ph, y], rows_send.at[ph, q], rows_recv.at[ph, y],
            device_id=on_y(q), device_id_type=MESH,
        )

    def rows_arrived(ph, q):
        return pltpu.make_async_remote_copy(
            rows_out.at[ph, q], rows_in.at[ph, q], rows_send.at[ph, q], rows_recv.at[ph, q],
            device_id=on_y(q), device_id_type=MESH,
        )

    def back_copy(ph, q):
        return pltpu.make_async_remote_copy(
            rows_in.at[ph, q], back_in.at[ph, y], back_send.at[ph, q], back_recv.at[ph, y],
            device_id=on_y(q), device_id_type=MESH,
        )

    def back_arrived(ph, q):
        return pltpu.make_async_remote_copy(
            rows_in.at[ph, q], back_in.at[ph, q], back_send.at[ph, q], back_recv.at[ph, q],
            device_id=on_y(q), device_id_type=MESH,
        )

    line_tok = LINE * tok
    slot_row = lax.broadcasted_iota(jnp.int32, (chunk, line_tok), 0).astype(F32)

    def send_rows(ph):
        def step(i, carry):
            q = (y + 1 + i) % planes
            match = slot_row == target[ph, pl.ds(q, 1), :]
            rows = dot(
                jnp.where(match, 1.0, 0.0).astype(BF16),
                jnp.concatenate([gathered[ph, zs] for zs in range(LINE)], axis=1),
                ((1,), (1,)),
            )
            if ph == 1:
                rows = rows * jnp.sum(
                    jnp.where(match, weight[ph, pl.ds(q, 1), :], 0.0), axis=1, keepdims=True
                )
            rows_out[ph, q] = rows.astype(BF16)

            @pl.when(i < planes - 1)
            def _():
                rows_copy(ph, q).start()
            return carry

        lax.fori_loop(0, planes, step, 0)
        rows_in[ph, y] = rows_out[ph, y]

    hop(0, 3)
    send_rows(0)

    @pl.when(ends)
    def _():
        rest_copy.start()
        coef_start(0)
        coef_start(1)

    hop(1, 1)
    hop(1, 2)

    @pl.when(inner)
    def _():
        rest_copy.start()
        coef_start(0)
        coef_start(1)

    hop(1, 3)
    send_rows(1)
    loads[1].wait()
    loads[2].wait()

    def forward_step(i, carry):
        q = (y + planes - i) % planes

        @pl.when(i > 0)
        def _():
            rows_arrived(0, q).wait_recv()

        both = dot(rows_in[0, q], win_ref[...])
        gate = both[:, :units]
        hidden = (gate * (1.0 / (1.0 + jnp.exp(-gate))) * both[:, units:]).astype(BF16)
        rows_in[0, q] = dot(hidden, wdown_ref[...]).astype(BF16)

        @pl.when(i > 0)
        def _():
            back_copy(0, q).start()
        return carry

    lax.fori_loop(0, planes, forward_step, 0)
    coef_start(2)
    coef_start(3)

    lane_row = lax.broadcasted_iota(jnp.int32, (line_tok, chunk), 1).astype(F32)
    column = lax.broadcasted_iota(jnp.int32, (line_tok, 8), 1)

    def combine(ph, first, last):
        def step(i, carry):
            q = (y + i) % planes

            @pl.when(i % planes > 0)
            def _():
                back_arrived(ph, q).wait_recv()

            place = jnp.sum(jnp.where(column == q, target_t[ph], 0.0), axis=1, keepdims=True)
            match = lane_row == place
            rows = back_in[ph, q]
            if ph == 0:
                prob = jnp.sum(jnp.where(column == q, weight_t[ph], 0.0), axis=1, keepdims=True)
                full = jnp.where(match, prob, 0.0)
                high = full.astype(BF16)
                rest = (full - high.astype(F32)).astype(BF16)
                value = dot(high, rows) + dot(rest, rows)
            else:
                value = dot(jnp.where(match, 1.0, 0.0).astype(BF16), rows)
            total[ph] += value.reshape(total.shape[1:])
            return carry

        lax.fori_loop(first, last, step, 0)

    def part_copy(ph, up, d):
        if up:
            return pltpu.make_async_remote_copy(
                part_out.at[ph, d], part_up.at[ph, d], part_send.at[ph, d], up_recv.at[ph, d],
                device_id=on_z(z + 1), device_id_type=MESH,
            )
        return pltpu.make_async_remote_copy(
            part_out.at[ph, d], part_down.at[ph, d], part_send.at[ph, d], down_recv.at[ph, d],
            device_id=on_z(z - 1), device_id_type=MESH,
        )

    def send_up(ph, d):
        @pl.when(z == 0)
        def _():
            part_out[ph, d] = total[ph, d].T.astype(BF16)

        @pl.when((z > 0) & (z < d))
        def _():
            part_copy(ph, True, d).wait_recv()
            part_out[ph, d] = (total[ph, d].T + part_up[ph, d].astype(F32)).astype(BF16)

        @pl.when(z < d)
        def _():
            part_copy(ph, True, d).start()

    def send_down(ph, d):
        @pl.when(z == LINE - 1)
        def _():
            part_out[ph, d] = total[ph, d].T.astype(BF16)

        @pl.when((z < LINE - 1) & (z > d))
        def _():
            part_copy(ph, False, d).wait_recv()
            part_out[ph, d] = (total[ph, d].T + part_down[ph, d].astype(F32)).astype(BF16)

        @pl.when(z > d)
        def _():
            part_copy(ph, False, d).start()

    def reduce_line(ph):
        for s in range(LINE - 1):
            @pl.when((z > 0) & (z < LINE // 2))
            def _():
                send_up(ph, LINE - 1 - s)
                send_down(ph, s)

            @pl.when((z >= LINE // 2) & (z < LINE - 1))
            def _():
                send_down(ph, s)
                send_up(ph, LINE - 1 - s)

    def reduce_ends(ph):
        @pl.when(z == 0)
        def _():
            for s in range(LINE - 1):
                send_up(ph, LINE - 1 - s)

        @pl.when(z == LINE - 1)
        def _():
            for s in range(LINE - 1):
                send_down(ph, s)

    def finish_line(ph, out_ref):
        final[...] = total[ph, z].T

        @pl.when(z > 0)
        def _():
            part_copy(ph, True, z).wait_recv()
            final[...] += part_up[ph, z].astype(F32)

        @pl.when(z < LINE - 1)
        def _():
            part_copy(ph, False, z).wait_recv()
            final[...] += part_down[ph, z].astype(F32)

        out_ref[...] = final[...].astype(BF16)

    def rest_of(q):
        full = rest_in[...].astype(F32)
        picked = full[:, :rest]
        for n in range(1, planes):
            picked = jnp.where(q == n, full[:, n * rest : (n + 1) * rest], picked)
        return picked

    rest_copy.wait_recv()

    def backward_step(i, carry):
        q = (y + 2 * planes - 1 - i) % planes

        @pl.when(i < planes - 1)
        def _():
            rows_arrived(1, q).wait_recv()

        hidden = dot(rows_in[1, q], wdown_ref[...], ((1,), (1,)))
        coef_copy(q).wait_recv()
        ending = coef_in[q, :, 2 * main : body].astype(F32)
        tail = units - main
        joined = jnp.concatenate(
            [
                hidden[:, :main] * coef_in[q, :, 0:main].astype(F32),
                hidden[:, main:] * ending[:, :tail],
                hidden[:, :main] * coef_in[q, :, main : 2 * main].astype(F32),
                hidden[:, main : units - rest] * ending[:, tail:],
                hidden[:, units - rest :] * rest_of(q),
            ],
            axis=1,
        ).astype(BF16)
        rows_in[1, q] = dot(joined, win_ref[...], ((1,), (1,))).astype(BF16)

        @pl.when(i < planes - 1)
        def _():
            back_copy(1, q).start()
        return carry

    lax.fori_loop(0, 2, backward_step, 0)
    back_in[0, y] = rows_in[0, y]
    total[...] = jnp.zeros_like(total)
    combine(0, 0, planes)
    reduce_ends(0)
    lax.fori_loop(2, 3, backward_step, 0)
    combine(1, 1, planes)
    lax.fori_loop(3, planes, backward_step, 0)
    back_in[1, y] = rows_in[1, y]
    combine(1, planes, planes + 1)
    reduce_ends(1)
    reduce_line(0)
    reduce_line(1)
    finish_line(0, moe_ref)
    finish_line(1, gin_ref)

    for kind in range(3):
        hop_done(kind)
    rest_copy.wait_send()
    for q in range(planes):
        coef_copy(q).wait_send()
    for ph in range(2):
        for i in range(1, planes):
            rows_copy(ph, (y + i) % planes).wait_send()
            back_copy(ph, (y + i) % planes).wait_send()
        for d in range(LINE):
            @pl.when(z < d)
            def _():
                part_copy(ph, True, d).wait_send()

            @pl.when(z > d)
            def _():
                part_copy(ph, False, d).wait_send()


def local(
    tokens,
    routes_fwd,
    probs_fwd,
    grad_out,
    routes_bwd,
    probs_bwd,
    w_in,
    w_down,
    saved_codes,
    saved_scales,
    saved_exponent,
):
    devices = lax.axis_size("expert")
    planes = devices // LINE
    tok, depth = tokens.shape[1:]
    units = w_down.shape[2]
    rows = saved_codes.shape[1]
    cap = rows // devices
    chunk = cap * LINE
    body = 2 * units // 128 * 128
    rest = 2 * units - body
    block = 2 * units // saved_scales.shape[2]
    sizes = (lax.axis_size("pipe"), planes, cap, chunk, tok, units, block)
    vmem = pl.BlockSpec(memory_space=pltpu.VMEM)
    dma = pltpu.SemaphoreType.DMA
    moe, gin = pl.pallas_call(
        functools.partial(kernel, sizes),
        out_shape=[jax.ShapeDtypeStruct((depth, tok), BF16)] * 2,
        in_specs=[vmem] * 6 + [pl.BlockSpec(memory_space=pl.ANY)] * 3 + [vmem] * 2,
        out_specs=[vmem] * 2,
        scratch_shapes=[
            pltpu.VMEM((depth, 2 * units), BF16),
            pltpu.VMEM((units, depth), BF16),
            pltpu.VMEM((2 * units, rows), BF16),
            pltpu.VMEM((depth, tok), F32),
            pltpu.VMEM((rows, rest), BF16),
            dma((3,)),
            pltpu.VMEM((LINE, 16, tok), F32),
            pltpu.VMEM((2, LINE, depth, tok), BF16),
            pltpu.VMEM((2, 8, LINE * tok), F32),
            pltpu.VMEM((2, 8, LINE * tok), F32),
            pltpu.VMEM((2, LINE * tok, 8), F32),
            pltpu.VMEM((2, LINE * tok, 8), F32),
            pltpu.VMEM((rows, body), BF16),
            pltpu.VMEM((planes, chunk, body), BF16),
            pltpu.VMEM((chunk, planes * rest), BF16),
            pltpu.VMEM((chunk, planes * rest), BF16),
            pltpu.VMEM((2, planes, chunk, depth), BF16),
            pltpu.VMEM((2, planes, chunk, depth), BF16),
            pltpu.VMEM((2, planes, chunk, depth), BF16),
            pltpu.VMEM((2, LINE, tok, depth), F32),
            pltpu.VMEM((2, LINE, depth, tok), BF16),
            pltpu.VMEM((2, LINE, depth, tok), BF16),
            pltpu.VMEM((2, LINE, depth, tok), BF16),
            dma((2, LINE)),
            dma((LINE,)),
            dma((2, 2, LINE)),
            dma((2, LINE)),
            dma((planes,)),
            dma((planes,)),
            dma,
            dma,
            dma((2, planes)),
            dma((2, planes)),
            dma((2, planes)),
            dma((2, planes)),
            dma((2, LINE)),
            dma((2, LINE)),
            dma((2, LINE)),
        ],
        compiler_params=pltpu.CompilerParams(
            collective_id=0, has_side_effects=True, vmem_limit_bytes=62 << 20
        ),
        cost_estimate=pl.CostEstimate(
            flops=8 * rows * units * depth * 3, bytes_accessed=16 << 20, transcendentals=0
        ),
    )(
        routes_fwd[0].T,
        probs_fwd[0].T,
        routes_bwd[0].T,
        probs_bwd[0].T,
        tokens[0].T,
        grad_out[0].T,
        w_in[0, 0],
        w_down[0, 0],
        saved_codes[0].T,
        saved_scales[0].T,
        saved_exponent,
    )
    return (moe.T[None], gin.T[None])


def solution(mesh):
    rows3 = P("pipe", "expert", None)
    rows4 = P("pipe", "expert", None, None)
    in_specs = (rows3,) * 6 + (rows4, rows4, rows3, rows3, P("pipe", "expert"))
    return jax.shard_map(
        local, mesh=mesh, in_specs=in_specs, out_specs=(rows3, rows3), check_vma=False
    )
```

```python
import functools
import jax
import jax.numpy as jnp
from jax import lax
from jax.sharding import PartitionSpec as P
from jax.experimental import pallas as pl
from jax.experimental.pallas import tpu as pltpu

MESH = pl.DeviceIdType.MESH
LINE = 4
BF16 = jnp.bfloat16
F32 = jnp.float32


def dot(a, b, dims=((1,), (0,))):
    return lax.dot_general(a, b, (dims, ((), ())), preferred_element_type=F32)


def kernel(
    sizes,
    route_now_ref,
    prob_now_ref,
    route_old_ref,
    prob_old_ref,
    tok_ref,
    grad_ref,
    win_hbm,
    wdown_hbm,
    codes_hbm,
    scales_ref,
    exp_ref,
    out_ref,
    win_ref,
    wdown_ref,
    codes_ref,
    final,
    rest_all,
    load_sem,
    tabs,
    gathered,
    target,
    weight,
    target_t,
    weight_t,
    coef_out,
    coef_in,
    rest_out,
    rest_in,
    rows_out,
    rows_in,
    back_in,
    total,
    turned,
    part_out,
    part_up,
    part_down,
    tab_send,
    tab_recv,
    tok_send,
    tok_recv,
    coef_send,
    coef_recv,
    rest_send,
    rest_recv,
    rows_send,
    rows_recv,
    back_send,
    back_recv,
    part_send,
    up_recv,
    down_recv,
):
    pipes, planes, cap, chunk, tok, units, block = sizes
    main = units // 128 * 128
    body = 2 * units // 128 * 128
    rest = 2 * units - body
    p = lax.axis_index("pipe")
    e = lax.axis_index("expert")
    y = e // LINE
    z = e % LINE

    def on_z(q):
        return (p, y * LINE + q)

    def on_y(q):
        return (p, q * LINE + z)

    mirror = (pipes - 1 - p, e)

    loads = [
        pltpu.make_async_copy(src, dst, load_sem.at[n])
        for n, (src, dst) in enumerate(
            ((codes_hbm, codes_ref), (win_hbm, win_ref), (wdown_hbm, wdown_ref))
        )
    ]
    for load in loads:
        load.start()

    for n, part in enumerate((route_now_ref, prob_now_ref, route_old_ref, prob_old_ref)):
        tabs[z, 4 * n : 4 * n + 4, :] = part[...].astype(F32)
    gathered[0, z] = tok_ref[...]
    gathered[1, z] = grad_ref[...]

    bar = pltpu.get_barrier_semaphore()
    pl.semaphore_signal(bar, inc=1, device_id=mirror, device_id_type=MESH)
    for i in range(1, planes):
        pl.semaphore_signal(bar, inc=1, device_id=on_y((y + i) % planes), device_id_type=MESH)

    @pl.when(z > 0)
    def _():
        pl.semaphore_signal(bar, inc=1, device_id=on_z(z - 1), device_id_type=MESH)

    @pl.when(z < LINE - 1)
    def _():
        pl.semaphore_signal(bar, inc=1, device_id=on_z(z + 1), device_id_type=MESH)

    @pl.when((z > 0) & (z < LINE - 1))
    def _():
        pl.semaphore_wait(bar, planes + 2)

    @pl.when((z == 0) | (z == LINE - 1))
    def _():
        pl.semaphore_wait(bar, planes + 1)

    def hop_copy(kind, up, zs):
        to = on_z(z + 1) if up else on_z(z - 1)
        way = 0 if up else 1
        if kind == 2:
            return pltpu.make_async_remote_copy(
                tabs.at[zs], tabs.at[zs], tab_send.at[way, zs], tab_recv.at[zs],
                device_id=to, device_id_type=MESH,
            )
        return pltpu.make_async_remote_copy(
            gathered.at[kind, zs], gathered.at[kind, zs], tok_send.at[kind, way, zs],
            tok_recv.at[kind, zs], device_id=to, device_id_type=MESH,
        )

    def hop(kind, d):
        if d == 0:
            @pl.when(z < LINE - 1)
            def _():
                hop_copy(kind, True, z).start()

            @pl.when(z > 0)
            def _():
                hop_copy(kind, False, z).start()
            return

        @pl.when(z >= d)
        def _():
            hop_copy(kind, True, z - d).wait_recv()

            @pl.when(z < LINE - 1)
            def _():
                hop_copy(kind, True, z - d).start()

        @pl.when(z + d <= LINE - 1)
        def _():
            hop_copy(kind, False, z + d).wait_recv()

            @pl.when(z > 0)
            def _():
                hop_copy(kind, False, z + d).start()

    def hop_done(kind):
        for d in range(LINE - 1):
            @pl.when((z < LINE - 1) & (z >= d))
            def _():
                hop_copy(kind, True, z - d).wait_send()

            @pl.when((z > 0) & (z + d <= LINE - 1))
            def _():
                hop_copy(kind, False, z + d).wait_send()

    inner = (z > 0) & (z < LINE - 1)
    ends = (z == 0) | (z == LINE - 1)
    hop(2, 0)
    hop(0, 0)

    @pl.when(ends)
    def _():
        hop(1, 0)

    def coef_copy(q):
        return pltpu.make_async_remote_copy(
            coef_out.at[pl.ds(pl.multiple_of(q * chunk, 16), chunk)], coef_in.at[q], coef_send.at[q], coef_recv.at[q],
            device_id=mirror, device_id_type=MESH,
        )

    blocks = scales_ref.shape[0]
    low = lax.broadcasted_iota(jnp.int32, (2 * units, blocks), 1) * block
    line = lax.broadcasted_iota(jnp.int32, (2 * units, blocks), 0)
    spread = jnp.where((line >= low) & (line < low + block), 1.0, 0.0).astype(BF16)
    level = exp_ref[...]
    factor = jnp.zeros(level.shape, F32)
    for n in range(-2, 2):
        factor = factor + jnp.where(level == n, F32(2.0**n), F32(0.0))

    def coef_tile(start, size):
        here = pl.ds(start, size)
        value = codes_ref[:, here].astype(F32) * (dot(spread, scales_ref[:, here]) * factor)
        gate = value[:units]
        up = value[units:]
        sig = 1.0 / (1.0 + jnp.exp(-gate))
        one = (up * sig * (1.0 + gate * (1.0 - sig))).T
        two = (gate * sig).T
        coef_out[here, 0:main] = one[:, :main].astype(BF16)
        coef_out[here, main : 2 * main] = two[:, :main].astype(BF16)
        ending = jnp.concatenate([one[:, main:], two[:, main:]], axis=1)
        coef_out[here, 2 * main : body] = ending[:, : body - 2 * main].astype(BF16)
        rest_all[here, :] = ending[:, body - 2 * main :].astype(BF16)

    def coef_step(t, carry):
        coef_tile(pl.multiple_of(t * 128, 128), 128)
        return carry

    def coef_start(i):
        coef_copy((y + 2 * planes - 1 - i) % planes).start()

    rest_copy = pltpu.make_async_remote_copy(
        rest_out, rest_in, rest_send, rest_recv, device_id=mirror, device_id_type=MESH
    )
    loads[0].wait()
    rows = codes_ref.shape[1]
    half = rows // 256
    lax.fori_loop(0, half, coef_step, 0)
    hop(2, 1)
    hop(0, 1)

    @pl.when(inner)
    def _():
        hop(1, 0)

    lax.fori_loop(half, rows // 128, coef_step, 0)
    if rows % 128:
        coef_tile(rows // 128 * 128, rows % 128)
    rest_out[...] = jnp.concatenate(
        [rest_all[q * chunk : (q + 1) * chunk, :] for q in range(planes)], axis=1
    )

    hop(2, 2)
    hop(0, 2)
    hop(2, 3)

    plane_expert = (
        2 * lax.broadcasted_iota(jnp.int32, (8, tok), 0) + z // 2
    ).astype(F32)
    earlier = jnp.where(
        lax.broadcasted_iota(jnp.int32, (tok, tok), 0)
        < lax.broadcasted_iota(jnp.int32, (tok, tok), 1),
        1.0,
        0.0,
    ).astype(BF16)
    for ph in range(2):
        for zs in range(LINE):
            member = jnp.zeros((8, tok), F32)
            prob = jnp.zeros((8, tok), F32)
            for k in range(4):
                hit = tabs[zs, 8 * ph + k : 8 * ph + k + 1, :] == plane_expert
                member = member + jnp.where(hit, 1.0, 0.0)
                prob = prob + jnp.where(hit, tabs[zs, 8 * ph + 4 + k : 8 * ph + 5 + k, :], 0.0)
            before = dot(member.astype(BF16), earlier)
            target[ph, :, zs * tok : (zs + 1) * tok] = jnp.where(
                member > 0.5, before + F32(zs * cap), F32(-1.0)
            )
            weight[ph, :, zs * tok : (zs + 1) * tok] = prob
        target_t[ph] = target[ph].T
        weight_t[ph] = weight[ph].T

    def rows_copy(ph, q):
        return pltpu.make_async_remote_copy(
            rows_out.at[ph, q], rows_in.at[ph, y], rows_send.at[ph, q], rows_recv.at[ph, y],
            device_id=on_y(q), device_id_type=MESH,
        )

    def rows_arrived(ph, q):
        return pltpu.make_async_remote_copy(
            rows_out.at[ph, q], rows_in.at[ph, q], rows_send.at[ph, q], rows_recv.at[ph, q],
            device_id=on_y(q), device_id_type=MESH,
        )

    def back_copy(ph, q):
        return pltpu.make_async_remote_copy(
            rows_in.at[ph, q], back_in.at[ph, y], back_send.at[ph, q], back_recv.at[ph, y],
            device_id=on_y(q), device_id_type=MESH,
        )

    def back_arrived(ph, q):
        return pltpu.make_async_remote_copy(
            rows_in.at[ph, q], back_in.at[ph, q], back_send.at[ph, q], back_recv.at[ph, q],
            device_id=on_y(q), device_id_type=MESH,
        )

    line_tok = LINE * tok
    slot_row = lax.broadcasted_iota(jnp.int32, (chunk, line_tok), 0).astype(F32)

    def send_rows(ph):
        def step(i, carry):
            q = (y + 1 + i) % planes
            match = slot_row == target[ph, pl.ds(q, 1), :]
            rows = dot(
                jnp.where(match, 1.0, 0.0).astype(BF16),
                jnp.concatenate([gathered[ph, zs] for zs in range(LINE)], axis=1),
                ((1,), (1,)),
            )
            if ph == 1:
                rows = rows * jnp.sum(
                    jnp.where(match, weight[ph, pl.ds(q, 1), :], 0.0), axis=1, keepdims=True
                )
            rows_out[ph, q] = rows.astype(BF16)

            @pl.when(i < planes - 1)
            def _():
                rows_copy(ph, q).start()
            return carry

        lax.fori_loop(0, planes, step, 0)
        rows_in[ph, y] = rows_out[ph, y]

    hop(0, 3)
    send_rows(0)

    @pl.when(ends)
    def _():
        rest_copy.start()
        coef_start(0)
        coef_start(1)

    hop(1, 1)
    hop(1, 2)

    @pl.when(inner)
    def _():
        rest_copy.start()
        coef_start(0)
        coef_start(1)

    hop(1, 3)
    send_rows(1)
    loads[1].wait()
    loads[2].wait()

    def forward_step(i, carry):
        q = (y + planes - i) % planes

        @pl.when(i > 0)
        def _():
            rows_arrived(0, q).wait_recv()

        both = dot(rows_in[0, q], win_ref[...])
        gate = both[:, :units]
        hidden = (gate * (1.0 / (1.0 + jnp.exp(-gate))) * both[:, units:]).astype(BF16)
        rows_in[0, q] = dot(hidden, wdown_ref[...]).astype(BF16)

        @pl.when(i > 0)
        def _():
            back_copy(0, q).start()
        return carry

    lax.fori_loop(0, planes, forward_step, 0)
    coef_start(2)
    coef_start(3)

    lane_row = lax.broadcasted_iota(jnp.int32, (line_tok, chunk), 1).astype(F32)
    column = lax.broadcasted_iota(jnp.int32, (line_tok, 8), 1)

    def combine(ph, first, last):
        def step(i, carry):
            q = (y + i) % planes

            @pl.when(i % planes > 0)
            def _():
                back_arrived(ph, q).wait_recv()

            place = jnp.sum(jnp.where(column == q, target_t[ph], 0.0), axis=1, keepdims=True)
            match = lane_row == place
            rows = back_in[ph, q]
            if ph == 0:
                prob = jnp.sum(jnp.where(column == q, weight_t[ph], 0.0), axis=1, keepdims=True)
                full = jnp.where(match, prob, 0.0)
                high = full.astype(BF16)
                rest = (full - high.astype(F32)).astype(BF16)
                value = dot(high, rows) + dot(rest, rows)
            else:
                value = dot(jnp.where(match, 1.0, 0.0).astype(BF16), rows)
            total[...] += value.reshape(total.shape)
            return carry

        lax.fori_loop(first, last, step, 0)

    def turn(ph):
        for d in range(LINE):
            turned[ph, d] = total[d].T

    def part_copy(ph, up, d):
        if up:
            return pltpu.make_async_remote_copy(
                part_out.at[ph, d], part_up.at[ph, d], part_send.at[ph, d], up_recv.at[ph, d],
                device_id=on_z(z + 1), device_id_type=MESH,
            )
        return pltpu.make_async_remote_copy(
            part_out.at[ph, d], part_down.at[ph, d], part_send.at[ph, d], down_recv.at[ph, d],
            device_id=on_z(z - 1), device_id_type=MESH,
        )

    def send_up(ph, d):
        @pl.when(z == 0)
        def _():
            part_out[ph, d] = total[d].T.astype(BF16)

        @pl.when((z > 0) & (z < d))
        def _():
            part_copy(ph, True, d).wait_recv()
            part_out[ph, d] = (turned[ph, d] + part_up[ph, d].astype(F32)).astype(BF16)

        @pl.when(z < d)
        def _():
            part_copy(ph, True, d).start()

    def send_down(ph, d):
        @pl.when(z == LINE - 1)
        def _():
            part_out[ph, d] = total[d].T.astype(BF16)

        @pl.when((z < LINE - 1) & (z > d))
        def _():
            part_copy(ph, False, d).wait_recv()
            part_out[ph, d] = (turned[ph, d] + part_down[ph, d].astype(F32)).astype(BF16)

        @pl.when(z > d)
        def _():
            part_copy(ph, False, d).start()

    def reduce_line(ph):
        for s in range(LINE - 1):
            @pl.when((z > 0) & (z < LINE // 2))
            def _():
                send_up(ph, LINE - 1 - s)
                send_down(ph, s)

            @pl.when((z >= LINE // 2) & (z < LINE - 1))
            def _():
                send_down(ph, s)
                send_up(ph, LINE - 1 - s)

    def reduce_ends(ph):
        @pl.when(z == 0)
        def _():
            for s in range(LINE - 1):
                send_up(ph, LINE - 1 - s)

        @pl.when(z == LINE - 1)
        def _():
            for s in range(LINE - 1):
                send_down(ph, s)

    def finish_line(ph):
        final[...] = turned[ph, z]

        @pl.when(z > 0)
        def _():
            part_copy(ph, True, z).wait_recv()
            final[...] += part_up[ph, z].astype(F32)

        @pl.when(z < LINE - 1)
        def _():
            part_copy(ph, False, z).wait_recv()
            final[...] += part_down[ph, z].astype(F32)

        out_ref[ph] = final[...].astype(BF16)

    def rest_of(q):
        full = rest_in[...].astype(F32)
        picked = full[:, :rest]
        for n in range(1, planes):
            picked = jnp.where(q == n, full[:, n * rest : (n + 1) * rest], picked)
        return picked

    rest_copy.wait_recv()

    def backward_step(i, carry):
        q = (y + 2 * planes - 1 - i) % planes

        @pl.when(i < planes - 1)
        def _():
            rows_arrived(1, q).wait_recv()

        hidden = dot(rows_in[1, q], wdown_ref[...], ((1,), (1,)))
        coef_copy(q).wait_recv()
        ending = coef_in[q, :, 2 * main : body].astype(F32)
        tail = units - main
        joined = jnp.concatenate(
            [
                hidden[:, :main] * coef_in[q, :, 0:main].astype(F32),
                hidden[:, main:] * ending[:, :tail],
                hidden[:, :main] * coef_in[q, :, main : 2 * main].astype(F32),
                hidden[:, main : units - rest] * ending[:, tail:],
                hidden[:, units - rest :] * rest_of(q),
            ],
            axis=1,
        ).astype(BF16)
        rows_in[1, q] = dot(joined, win_ref[...], ((1,), (1,))).astype(BF16)

        @pl.when(i < planes - 1)
        def _():
            back_copy(1, q).start()
        return carry

    lax.fori_loop(0, 2, backward_step, 0)
    back_in[0, y] = rows_in[0, y]
    total[...] = jnp.zeros_like(total)
    combine(0, 0, planes)
    reduce_ends(0)
    turn(0)
    lax.fori_loop(2, 3, backward_step, 0)
    total[...] = jnp.zeros_like(total)
    combine(1, 1, planes)
    lax.fori_loop(3, planes, backward_step, 0)
    back_in[1, y] = rows_in[1, y]
    combine(1, planes, planes + 1)
    reduce_ends(1)
    turn(1)
    reduce_line(0)
    reduce_line(1)
    finish_line(0)
    finish_line(1)

    for kind in range(3):
        hop_done(kind)
    rest_copy.wait_send()
    for q in range(planes):
        coef_copy(q).wait_send()
    for ph in range(2):
        for i in range(1, planes):
            rows_copy(ph, (y + i) % planes).wait_send()
            back_copy(ph, (y + i) % planes).wait_send()
        for d in range(LINE):
            @pl.when(z < d)
            def _():
                part_copy(ph, True, d).wait_send()

            @pl.when(z > d)
            def _():
                part_copy(ph, False, d).wait_send()


def local(
    tokens,
    routes_fwd,
    probs_fwd,
    grad_out,
    routes_bwd,
    probs_bwd,
    w_in,
    w_down,
    saved_codes,
    saved_scales,
    saved_exponent,
):
    devices = lax.axis_size("expert")
    planes = devices // LINE
    tok, depth = tokens.shape[1:]
    units = w_down.shape[2]
    rows = saved_codes.shape[1]
    cap = rows // devices
    chunk = cap * LINE
    body = 2 * units // 128 * 128
    rest = 2 * units - body
    block = 2 * units // saved_scales.shape[2]
    sizes = (lax.axis_size("pipe"), planes, cap, chunk, tok, units, block)
    vmem = pl.BlockSpec(memory_space=pltpu.VMEM)
    dma = pltpu.SemaphoreType.DMA
    out = pl.pallas_call(
        functools.partial(kernel, sizes),
        out_shape=jax.ShapeDtypeStruct((2, depth, tok), BF16),
        in_specs=[vmem] * 6 + [pl.BlockSpec(memory_space=pl.ANY)] * 3 + [vmem] * 2,
        out_specs=vmem,
        scratch_shapes=[
            pltpu.VMEM((depth, 2 * units), BF16),
            pltpu.VMEM((units, depth), BF16),
            pltpu.VMEM((2 * units, rows), BF16),
            pltpu.VMEM((depth, tok), F32),
            pltpu.VMEM((rows, rest), BF16),
            dma((3,)),
            pltpu.VMEM((LINE, 16, tok), F32),
            pltpu.VMEM((2, LINE, depth, tok), BF16),
            pltpu.VMEM((2, 8, LINE * tok), F32),
            pltpu.VMEM((2, 8, LINE * tok), F32),
            pltpu.VMEM((2, LINE * tok, 8), F32),
            pltpu.VMEM((2, LINE * tok, 8), F32),
            pltpu.VMEM((rows, body), BF16),
            pltpu.VMEM((planes, chunk, body), BF16),
            pltpu.VMEM((chunk, planes * rest), BF16),
            pltpu.VMEM((chunk, planes * rest), BF16),
            pltpu.VMEM((2, planes, chunk, depth), BF16),
            pltpu.VMEM((2, planes, chunk, depth), BF16),
            pltpu.VMEM((2, planes, chunk, depth), BF16),
            pltpu.VMEM((LINE, tok, depth), F32),
            pltpu.VMEM((2, LINE, depth, tok), F32),
            pltpu.VMEM((2, LINE, depth, tok), BF16),
            pltpu.VMEM((2, LINE, depth, tok), BF16),
            pltpu.VMEM((2, LINE, depth, tok), BF16),
            dma((2, LINE)),
            dma((LINE,)),
            dma((2, 2, LINE)),
            dma((2, LINE)),
            dma((planes,)),
            dma((planes,)),
            dma,
            dma,
            dma((2, planes)),
            dma((2, planes)),
            dma((2, planes)),
            dma((2, planes)),
            dma((2, LINE)),
            dma((2, LINE)),
            dma((2, LINE)),
        ],
        compiler_params=pltpu.CompilerParams(
            collective_id=0, has_side_effects=True, vmem_limit_bytes=62 << 20
        ),
        cost_estimate=pl.CostEstimate(
            flops=8 * rows * units * depth * 3, bytes_accessed=16 << 20, transcendentals=0
        ),
    )(
        routes_fwd[0].T,
        probs_fwd[0].T,
        routes_bwd[0].T,
        probs_bwd[0].T,
        tokens[0].T,
        grad_out[0].T,
        w_in[0, 0],
        w_down[0, 0],
        saved_codes[0].T,
        saved_scales[0].T,
        saved_exponent,
    )
    return (out[0].T[None], out[1].T[None])


def solution(mesh):
    rows3 = P("pipe", "expert", None)
    rows4 = P("pipe", "expert", None, None)
    in_specs = (rows3,) * 6 + (rows4, rows4, rows3, rows3, P("pipe", "expert"))
    return jax.shard_map(
        local, mesh=mesh, in_specs=in_specs, out_specs=(rows3, rows3), check_vma=False
    )
```

```python
import functools
import jax
import jax.numpy as jnp
from jax import lax
from jax.sharding import PartitionSpec as P
from jax.experimental import pallas as pl
from jax.experimental.pallas import tpu as pltpu

MESH = pl.DeviceIdType.MESH
LINE = 4
BF16 = jnp.bfloat16
F32 = jnp.float32


def dot(a, b, dims=((1,), (0,))):
    return lax.dot_general(a, b, (dims, ((), ())), preferred_element_type=F32)


def kernel(
    sizes,
    route_now_ref,
    prob_now_ref,
    route_old_ref,
    prob_old_ref,
    tok_ref,
    grad_ref,
    win_hbm,
    wdown_hbm,
    codes_hbm,
    scales_ref,
    exp_ref,
    out_ref,
    win_ref,
    wdown_ref,
    codes_ref,
    final,
    rest_all,
    load_sem,
    tabs,
    gathered,
    target,
    weight,
    target_t,
    weight_t,
    coef_out,
    coef_in,
    rest_out,
    rest_in,
    rows_out,
    rows_in,
    back_in,
    total,
    turned,
    part_out,
    part_up,
    part_down,
    tab_send,
    tab_recv,
    tok_send,
    tok_recv,
    coef_send,
    coef_recv,
    rest_send,
    rest_recv,
    rows_send,
    rows_recv,
    back_send,
    back_recv,
    part_send,
    up_recv,
    down_recv,
):
    pipes, planes, cap, chunk, tok, units, block = sizes
    main = units // 128 * 128
    body = 2 * units // 128 * 128
    rest = 2 * units - body
    p = lax.axis_index("pipe")
    e = lax.axis_index("expert")
    y = e // LINE
    z = e % LINE

    def on_z(q):
        return (p, y * LINE + q)

    def on_y(q):
        return (p, q * LINE + z)

    mirror = (pipes - 1 - p, e)

    loads = [
        pltpu.make_async_copy(src, dst, load_sem.at[n])
        for n, (src, dst) in enumerate(
            ((codes_hbm, codes_ref), (win_hbm, win_ref), (wdown_hbm, wdown_ref))
        )
    ]
    for load in loads:
        load.start()

    for n, part in enumerate((route_now_ref, prob_now_ref, route_old_ref, prob_old_ref)):
        tabs[z, 4 * n : 4 * n + 4, :] = part[...].astype(F32)
    gathered[0, z] = tok_ref[...]
    gathered[1, z] = grad_ref[...]

    bar = pltpu.get_barrier_semaphore()
    pl.semaphore_signal(bar, inc=1, device_id=mirror, device_id_type=MESH)
    for i in range(1, planes):
        pl.semaphore_signal(bar, inc=1, device_id=on_y((y + i) % planes), device_id_type=MESH)

    @pl.when(z > 0)
    def _():
        pl.semaphore_signal(bar, inc=1, device_id=on_z(z - 1), device_id_type=MESH)

    @pl.when(z < LINE - 1)
    def _():
        pl.semaphore_signal(bar, inc=1, device_id=on_z(z + 1), device_id_type=MESH)

    @pl.when((z > 0) & (z < LINE - 1))
    def _():
        pl.semaphore_wait(bar, planes + 2)

    @pl.when((z == 0) | (z == LINE - 1))
    def _():
        pl.semaphore_wait(bar, planes + 1)

    def hop_copy(kind, up, zs):
        to = on_z(z + 1) if up else on_z(z - 1)
        way = 0 if up else 1
        if kind == 2:
            return pltpu.make_async_remote_copy(
                tabs.at[zs], tabs.at[zs], tab_send.at[way, zs], tab_recv.at[zs],
                device_id=to, device_id_type=MESH,
            )
        return pltpu.make_async_remote_copy(
            gathered.at[kind, zs], gathered.at[kind, zs], tok_send.at[kind, way, zs],
            tok_recv.at[kind, zs], device_id=to, device_id_type=MESH,
        )

    def hop(kind, d):
        if d == 0:
            @pl.when(z < LINE - 1)
            def _():
                hop_copy(kind, True, z).start()

            @pl.when(z > 0)
            def _():
                hop_copy(kind, False, z).start()
            return

        @pl.when(z >= d)
        def _():
            hop_copy(kind, True, z - d).wait_recv()

            @pl.when(z < LINE - 1)
            def _():
                hop_copy(kind, True, z - d).start()

        @pl.when(z + d <= LINE - 1)
        def _():
            hop_copy(kind, False, z + d).wait_recv()

            @pl.when(z > 0)
            def _():
                hop_copy(kind, False, z + d).start()

    def hop_done(kind):
        for d in range(LINE - 1):
            @pl.when((z < LINE - 1) & (z >= d))
            def _():
                hop_copy(kind, True, z - d).wait_send()

            @pl.when((z > 0) & (z + d <= LINE - 1))
            def _():
                hop_copy(kind, False, z + d).wait_send()

    inner = (z > 0) & (z < LINE - 1)
    ends = (z == 0) | (z == LINE - 1)
    hop(2, 0)
    hop(0, 0)

    @pl.when(ends)
    def _():
        hop(1, 0)

    def coef_copy(q):
        return pltpu.make_async_remote_copy(
            coef_out.at[pl.ds(pl.multiple_of(q * chunk, 16), chunk)], coef_in.at[q], coef_send.at[q], coef_recv.at[q],
            device_id=mirror, device_id_type=MESH,
        )

    blocks = scales_ref.shape[0]
    low = lax.broadcasted_iota(jnp.int32, (2 * units, blocks), 1) * block
    line = lax.broadcasted_iota(jnp.int32, (2 * units, blocks), 0)
    spread = jnp.where((line >= low) & (line < low + block), 1.0, 0.0).astype(BF16)
    level = exp_ref[...]
    factor = jnp.zeros(level.shape, F32)
    for n in range(-2, 2):
        factor = factor + jnp.where(level == n, F32(2.0**n), F32(0.0))

    def coef_tile(start, size):
        here = pl.ds(start, size)
        value = codes_ref[:, here].astype(F32) * (dot(spread, scales_ref[:, here]) * factor)
        gate = value[:units]
        up = value[units:]
        sig = 1.0 / (1.0 + jnp.exp(-gate))
        one = (up * sig * (1.0 + gate * (1.0 - sig))).T
        two = (gate * sig).T
        coef_out[here, 0:main] = one[:, :main].astype(BF16)
        coef_out[here, main : 2 * main] = two[:, :main].astype(BF16)
        ending = jnp.concatenate([one[:, main:], two[:, main:]], axis=1)
        coef_out[here, 2 * main : body] = ending[:, : body - 2 * main].astype(BF16)
        rest_all[here, :] = ending[:, body - 2 * main :].astype(BF16)

    def coef_step(t, carry):
        coef_tile(pl.multiple_of(t * 128, 128), 128)
        return carry

    def coef_start(i):
        coef_copy((y + 2 * planes - 1 - i) % planes).start()

    rest_copy = pltpu.make_async_remote_copy(
        rest_out, rest_in, rest_send, rest_recv, device_id=mirror, device_id_type=MESH
    )
    loads[0].wait()
    rows = codes_ref.shape[1]
    half = rows // 256
    lax.fori_loop(0, half, coef_step, 0)
    hop(2, 1)
    hop(0, 1)

    @pl.when(inner)
    def _():
        hop(1, 0)

    lax.fori_loop(half, rows // 128, coef_step, 0)
    if rows % 128:
        coef_tile(rows // 128 * 128, rows % 128)
    rest_out[...] = jnp.concatenate(
        [rest_all[q * chunk : (q + 1) * chunk, :] for q in range(planes)], axis=1
    )

    hop(2, 2)
    hop(0, 2)
    hop(2, 3)

    @pl.when(ends)
    def _():
        rest_copy.start()
        coef_start(0)

    plane_expert = (
        2 * lax.broadcasted_iota(jnp.int32, (8, tok), 0) + z // 2
    ).astype(F32)
    earlier = jnp.where(
        lax.broadcasted_iota(jnp.int32, (tok, tok), 0)
        < lax.broadcasted_iota(jnp.int32, (tok, tok), 1),
        1.0,
        0.0,
    ).astype(BF16)
    for ph in range(2):
        for zs in range(LINE):
            member = jnp.zeros((8, tok), F32)
            prob = jnp.zeros((8, tok), F32)
            for k in range(4):
                hit = tabs[zs, 8 * ph + k : 8 * ph + k + 1, :] == plane_expert
                member = member + jnp.where(hit, 1.0, 0.0)
                prob = prob + jnp.where(hit, tabs[zs, 8 * ph + 4 + k : 8 * ph + 5 + k, :], 0.0)
            before = dot(member.astype(BF16), earlier)
            target[ph, :, zs * tok : (zs + 1) * tok] = jnp.where(
                member > 0.5, before + F32(zs * cap), F32(-1.0)
            )
            weight[ph, :, zs * tok : (zs + 1) * tok] = prob
        target_t[ph] = target[ph].T
        weight_t[ph] = weight[ph].T

    def rows_copy(ph, q):
        return pltpu.make_async_remote_copy(
            rows_out.at[ph, q], rows_in.at[ph, y], rows_send.at[ph, q], rows_recv.at[ph, y],
            device_id=on_y(q), device_id_type=MESH,
        )

    def rows_arrived(ph, q):
        return pltpu.make_async_remote_copy(
            rows_out.at[ph, q], rows_in.at[ph, q], rows_send.at[ph, q], rows_recv.at[ph, q],
            device_id=on_y(q), device_id_type=MESH,
        )

    def back_copy(ph, q):
        return pltpu.make_async_remote_copy(
            rows_in.at[ph, q], back_in.at[ph, y], back_send.at[ph, q], back_recv.at[ph, y],
            device_id=on_y(q), device_id_type=MESH,
        )

    def back_arrived(ph, q):
        return pltpu.make_async_remote_copy(
            rows_in.at[ph, q], back_in.at[ph, q], back_send.at[ph, q], back_recv.at[ph, q],
            device_id=on_y(q), device_id_type=MESH,
        )

    line_tok = LINE * tok
    slot_row = lax.broadcasted_iota(jnp.int32, (chunk, line_tok), 0).astype(F32)

    def send_rows(ph):
        def step(i, carry):
            q = (y + 1 + i) % planes
            match = slot_row == target[ph, pl.ds(q, 1), :]
            rows = dot(
                jnp.where(match, 1.0, 0.0).astype(BF16),
                jnp.concatenate([gathered[ph, zs] for zs in range(LINE)], axis=1),
                ((1,), (1,)),
            )
            if ph == 1:
                rows = rows * jnp.sum(
                    jnp.where(match, weight[ph, pl.ds(q, 1), :], 0.0), axis=1, keepdims=True
                )
            rows_out[ph, q] = rows.astype(BF16)

            @pl.when(i < planes - 1)
            def _():
                rows_copy(ph, q).start()
            return carry

        lax.fori_loop(0, planes, step, 0)
        rows_in[ph, y] = rows_out[ph, y]

    hop(0, 3)
    send_rows(0)

    @pl.when(ends)
    def _():
        coef_start(1)

    hop(1, 1)
    hop(1, 2)

    @pl.when(inner)
    def _():
        rest_copy.start()
        coef_start(0)
        coef_start(1)

    hop(1, 3)
    send_rows(1)
    loads[1].wait()
    loads[2].wait()

    def forward_step(i, carry):
        q = (y + planes - i) % planes

        @pl.when(i > 0)
        def _():
            rows_arrived(0, q).wait_recv()

        both = dot(rows_in[0, q], win_ref[...])
        gate = both[:, :units]
        hidden = (gate * (1.0 / (1.0 + jnp.exp(-gate))) * both[:, units:]).astype(BF16)
        rows_in[0, q] = dot(hidden, wdown_ref[...]).astype(BF16)

        @pl.when(i > 0)
        def _():
            back_copy(0, q).start()
        return carry

    lax.fori_loop(0, planes, forward_step, 0)
    coef_start(2)
    coef_start(3)

    lane_row = lax.broadcasted_iota(jnp.int32, (line_tok, chunk), 1).astype(F32)
    column = lax.broadcasted_iota(jnp.int32, (line_tok, 8), 1)

    def combine(ph, first, last):
        def step(i, carry):
            q = (y + i) % planes

            @pl.when(i % planes > 0)
            def _():
                back_arrived(ph, q).wait_recv()

            place = jnp.sum(jnp.where(column == q, target_t[ph], 0.0), axis=1, keepdims=True)
            match = lane_row == place
            rows = back_in[ph, q]
            if ph == 0:
                prob = jnp.sum(jnp.where(column == q, weight_t[ph], 0.0), axis=1, keepdims=True)
                full = jnp.where(match, prob, 0.0)
                high = full.astype(BF16)
                rest = (full - high.astype(F32)).astype(BF16)
                value = dot(high, rows) + dot(rest, rows)
            else:
                value = dot(jnp.where(match, 1.0, 0.0).astype(BF16), rows)
            total[...] += value.reshape(total.shape)
            return carry

        lax.fori_loop(first, last, step, 0)

    def turn(ph):
        for d in range(LINE):
            turned[ph, d] = total[d].T

    def part_copy(ph, up, d):
        if up:
            return pltpu.make_async_remote_copy(
                part_out.at[ph, d], part_up.at[ph, d], part_send.at[ph, d], up_recv.at[ph, d],
                device_id=on_z(z + 1), device_id_type=MESH,
            )
        return pltpu.make_async_remote_copy(
            part_out.at[ph, d], part_down.at[ph, d], part_send.at[ph, d], down_recv.at[ph, d],
            device_id=on_z(z - 1), device_id_type=MESH,
        )

    def send_up(ph, d):
        @pl.when(z == 0)
        def _():
            part_out[ph, d] = total[d].T.astype(BF16)

        @pl.when((z > 0) & (z < d))
        def _():
            part_copy(ph, True, d).wait_recv()
            part_out[ph, d] = (turned[ph, d] + part_up[ph, d].astype(F32)).astype(BF16)

        @pl.when(z < d)
        def _():
            part_copy(ph, True, d).start()

    def send_down(ph, d):
        @pl.when(z == LINE - 1)
        def _():
            part_out[ph, d] = total[d].T.astype(BF16)

        @pl.when((z < LINE - 1) & (z > d))
        def _():
            part_copy(ph, False, d).wait_recv()
            part_out[ph, d] = (turned[ph, d] + part_down[ph, d].astype(F32)).astype(BF16)

        @pl.when(z > d)
        def _():
            part_copy(ph, False, d).start()

    def reduce_line(ph):
        for s in range(LINE - 1):
            @pl.when((z > 0) & (z < LINE // 2))
            def _():
                send_up(ph, LINE - 1 - s)
                send_down(ph, s)

            @pl.when((z >= LINE // 2) & (z < LINE - 1))
            def _():
                send_down(ph, s)
                send_up(ph, LINE - 1 - s)

    def reduce_ends(ph):
        @pl.when(z == 0)
        def _():
            for s in range(LINE - 1):
                send_up(ph, LINE - 1 - s)

        @pl.when(z == LINE - 1)
        def _():
            for s in range(LINE - 1):
                send_down(ph, s)

    def finish_line(ph):
        final[...] = turned[ph, z]

        @pl.when(z > 0)
        def _():
            part_copy(ph, True, z).wait_recv()
            final[...] += part_up[ph, z].astype(F32)

        @pl.when(z < LINE - 1)
        def _():
            part_copy(ph, False, z).wait_recv()
            final[...] += part_down[ph, z].astype(F32)

        out_ref[ph] = final[...].astype(BF16)

    def rest_of(q):
        full = rest_in[...].astype(F32)
        picked = full[:, :rest]
        for n in range(1, planes):
            picked = jnp.where(q == n, full[:, n * rest : (n + 1) * rest], picked)
        return picked

    rest_copy.wait_recv()

    def backward_step(i, carry):
        q = (y + 2 * planes - 1 - i) % planes

        @pl.when(i < planes - 1)
        def _():
            rows_arrived(1, q).wait_recv()

        hidden = dot(rows_in[1, q], wdown_ref[...], ((1,), (1,)))
        coef_copy(q).wait_recv()
        ending = coef_in[q, :, 2 * main : body].astype(F32)
        tail = units - main
        joined = jnp.concatenate(
            [
                hidden[:, :main] * coef_in[q, :, 0:main].astype(F32),
                hidden[:, main:] * ending[:, :tail],
                hidden[:, :main] * coef_in[q, :, main : 2 * main].astype(F32),
                hidden[:, main : units - rest] * ending[:, tail:],
                hidden[:, units - rest :] * rest_of(q),
            ],
            axis=1,
        ).astype(BF16)
        rows_in[1, q] = dot(joined, win_ref[...], ((1,), (1,))).astype(BF16)

        @pl.when(i < planes - 1)
        def _():
            back_copy(1, q).start()
        return carry

    lax.fori_loop(0, 2, backward_step, 0)
    back_in[0, y] = rows_in[0, y]
    total[...] = jnp.zeros_like(total)
    combine(0, 0, planes)
    reduce_ends(0)
    turn(0)
    lax.fori_loop(2, 3, backward_step, 0)
    total[...] = jnp.zeros_like(total)
    combine(1, 1, planes)
    lax.fori_loop(3, planes, backward_step, 0)
    back_in[1, y] = rows_in[1, y]
    combine(1, planes, planes + 1)
    reduce_ends(1)
    turn(1)
    reduce_line(0)
    reduce_line(1)
    finish_line(0)
    finish_line(1)

    for kind in range(3):
        hop_done(kind)
    rest_copy.wait_send()
    for q in range(planes):
        coef_copy(q).wait_send()
    for ph in range(2):
        for i in range(1, planes):
            rows_copy(ph, (y + i) % planes).wait_send()
            back_copy(ph, (y + i) % planes).wait_send()
        for d in range(LINE):
            @pl.when(z < d)
            def _():
                part_copy(ph, True, d).wait_send()

            @pl.when(z > d)
            def _():
                part_copy(ph, False, d).wait_send()


def local(
    tokens,
    routes_fwd,
    probs_fwd,
    grad_out,
    routes_bwd,
    probs_bwd,
    w_in,
    w_down,
    saved_codes,
    saved_scales,
    saved_exponent,
):
    devices = lax.axis_size("expert")
    planes = devices // LINE
    tok, depth = tokens.shape[1:]
    units = w_down.shape[2]
    rows = saved_codes.shape[1]
    cap = rows // devices
    chunk = cap * LINE
    body = 2 * units // 128 * 128
    rest = 2 * units - body
    block = 2 * units // saved_scales.shape[2]
    sizes = (lax.axis_size("pipe"), planes, cap, chunk, tok, units, block)
    vmem = pl.BlockSpec(memory_space=pltpu.VMEM)
    dma = pltpu.SemaphoreType.DMA
    out = pl.pallas_call(
        functools.partial(kernel, sizes),
        out_shape=jax.ShapeDtypeStruct((2, depth, tok), BF16),
        in_specs=[vmem] * 6 + [pl.BlockSpec(memory_space=pl.ANY)] * 3 + [vmem] * 2,
        out_specs=vmem,
        scratch_shapes=[
            pltpu.VMEM((depth, 2 * units), BF16),
            pltpu.VMEM((units, depth), BF16),
            pltpu.VMEM((2 * units, rows), BF16),
            pltpu.VMEM((depth, tok), F32),
            pltpu.VMEM((rows, rest), BF16),
            dma((3,)),
            pltpu.VMEM((LINE, 16, tok), F32),
            pltpu.VMEM((2, LINE, depth, tok), BF16),
            pltpu.VMEM((2, 8, LINE * tok), F32),
            pltpu.VMEM((2, 8, LINE * tok), F32),
            pltpu.VMEM((2, LINE * tok, 8), F32),
            pltpu.VMEM((2, LINE * tok, 8), F32),
            pltpu.VMEM((rows, body), BF16),
            pltpu.VMEM((planes, chunk, body), BF16),
            pltpu.VMEM((chunk, planes * rest), BF16),
            pltpu.VMEM((chunk, planes * rest), BF16),
            pltpu.VMEM((2, planes, chunk, depth), BF16),
            pltpu.VMEM((2, planes, chunk, depth), BF16),
            pltpu.VMEM((2, planes, chunk, depth), BF16),
            pltpu.VMEM((LINE, tok, depth), F32),
            pltpu.VMEM((2, LINE, depth, tok), F32),
            pltpu.VMEM((2, LINE, depth, tok), BF16),
            pltpu.VMEM((2, LINE, depth, tok), BF16),
            pltpu.VMEM((2, LINE, depth, tok), BF16),
            dma((2, LINE)),
            dma((LINE,)),
            dma((2, 2, LINE)),
            dma((2, LINE)),
            dma((planes,)),
            dma((planes,)),
            dma,
            dma,
            dma((2, planes)),
            dma((2, planes)),
            dma((2, planes)),
            dma((2, planes)),
            dma((2, LINE)),
            dma((2, LINE)),
            dma((2, LINE)),
        ],
        compiler_params=pltpu.CompilerParams(
            collective_id=0, has_side_effects=True, vmem_limit_bytes=62 << 20
        ),
        cost_estimate=pl.CostEstimate(
            flops=8 * rows * units * depth * 3, bytes_accessed=16 << 20, transcendentals=0
        ),
    )(
        routes_fwd[0].T,
        probs_fwd[0].T,
        routes_bwd[0].T,
        probs_bwd[0].T,
        tokens[0].T,
        grad_out[0].T,
        w_in[0, 0],
        w_down[0, 0],
        saved_codes[0].T,
        saved_scales[0].T,
        saved_exponent,
    )
    return (out[0].T[None], out[1].T[None])


def solution(mesh):
    rows3 = P("pipe", "expert", None)
    rows4 = P("pipe", "expert", None, None)
    in_specs = (rows3,) * 6 + (rows4, rows4, rows3, rows3, P("pipe", "expert"))
    return jax.shard_map(
        local, mesh=mesh, in_specs=in_specs, out_specs=(rows3, rows3), check_vma=False
    )
```
